32 devices in a mesh: roll: 4 (over x, core), tp: 8 (over z, y).
Axes of the slice: x: 2, y: 2, z: 4, core: 2. Of those that a mesh axis runs over, the one named last changes fastest.
Arguments:
- tokens: bfloat16 [128, 8, 2048], P(('roll', 'tp')), may hold values from -6 to 6
- lengths: int32 [128], P(('roll', 'tp')), may hold values from 1 to 8
- plan: int32 [2, 128, 1], P(None, ('roll', 'tp')), may hold values from 0 to 3, as said below
- owners: int32 [4], replicated, may hold values from 0 to 3, each once
- gate_up: float32 [4, 8, 2048, 768], P('roll', 'tp'), may hold values from -0.125 to 0.125
- down: float32 [4, 8, 384, 2048], P('roll', 'tp'), may hold values from -0.3125 to 0.3125
- norm_gain: float32 [2, 2048], replicated, may hold values from 0.5 to 1.5
- routing: int32 [2, 2048, 1], P(None, ('roll', 'tp')), may hold values from 0 to 7; in each aligned block of 64 rows (0 to 63, 64 to 127, ..., all dimensions but the last counted through in order) at most 10 rows name the same one
- route_weight: float32 [2, 2048], P(None, ('roll', 'tp')), may hold values from 0.1 to 1
Outputs:
- result: bfloat16 [128, 8, 2048], P(('roll', 'tp'))
The draws below stay inside these ranges and needn't reach their ends.
Inputs may be any that keep to these rules, and one draw needn't show every extreme that they name: In layer 0 at most 2 rows of one device name the same owner, and every device's rows reach 2. For l >= 1, plan[l, i, 0] = (r + s_l[plan[l - 1, i, 0]]) mod 4, with r the roll index of row i's device and s_l a permutation of the owners drawn for layer l. owners is a permutation; layer l's master lies in the slot of roll index owners[l]. `routing`: every received token slot, empty ones included, names one window expert; of the 64 slots of one device at most 10 name the same expert, and in every draw some device reaches 10.
All inputs are finite; a program needn't handle non-finite values.
Results may differ from the reference program's by a relative error of at most 0.0048.
Values may be sent and summed in bfloat16 or wider, within the bound.
A program may use at most 128 MiB of HBM per device.

```python
import math
import jax
import jax.numpy as jnp
import numpy as np
from jax import lax

D = 2048
FF_WIN = 384
LAYERS = 2
TOPK = 1
CAP = 2
ROW_TOK = 8
ROWS_DEV = 4
ROWS = 128
RECV_TOK = 64
CAP_E = 10
N_ROLL = 4
N_TP = 8


def device_owners(key):
    first_key, second_key, third_key = jax.random.split(key, 3)
    favored = jax.random.randint(first_key, (), 0, N_ROLL, dtype=jnp.int32)
    pool = jnp.tile(jnp.arange(N_ROLL, dtype=jnp.int32), CAP)
    mixed = jax.random.permutation(second_key, pool)
    order = jnp.argsort((mixed == favored).astype(jnp.int32), stable=True)
    others = mixed[order][:ROWS_DEV - CAP]
    picked = jnp.concatenate([jnp.full((CAP,), favored, jnp.int32), others])
    return jax.random.permutation(third_key, picked)


def draw_plan(key, part):
    device_count = N_ROLL * N_TP
    device_keys = jax.random.split(jax.random.fold_in(key, 1), device_count)
    first_layer = jax.vmap(device_owners)(device_keys).reshape(-1).astype(jnp.int32)
    home_roll = jnp.arange(ROWS, dtype=jnp.int32) // ROWS_DEV // N_TP
    layers = [first_layer]
    for layer_index in range(1, LAYERS):
        shuffle = jax.random.permutation(jax.random.fold_in(key, 10 + layer_index), N_ROLL).astype(jnp.int32)
        layers.append(((home_roll + shuffle[layers[-1]]) % N_ROLL).astype(jnp.int32))
    return jnp.stack(layers, axis=0)[:, :, None]


def plant(drawn, own_key, low, largest):
    longest = drawn.shape.index(max(drawn.shape))
    spots = []
    for shift in (0, 1):
        where = [jax.random.randint(jax.random.fold_in(own_key, axis), (), 0, length) for axis, length in enumerate(drawn.shape)]
        where[longest] = (where[longest] + shift) % drawn.shape[longest]
        spots.append(tuple(where))
    return drawn.at[spots[0]].set(low).at[spots[1]].set(largest)


def steps_of(key, extent, cuts, least, largest):
    factor_of = 1.0
    for dim, shards_of in cuts:
        steps = jax.random.uniform(jax.random.fold_in(jax.random.fold_in(key, 6), dim), (shards_of,), jnp.float32, least / len(cuts), largest / len(cuts))
        factor_of = factor_of * jnp.repeat(jnp.exp(steps), extent[dim] // shards_of).reshape((-1,) + (1,) * (len(extent) - 1 - dim))
    return factor_of


def deal_out(own_key, own, number, rows, number_of, top, most, skew):
    order = jax.random.permutation(own_key, number_of)
    heavy_load, common = portions_of(number_of, rows * top, most, skew, True), portions_of(number_of, rows * top, most, skew, False)
    places = jnp.arange(number_of)

    def named(sizes, offset_by):
        used = int((sizes > 0).sum())
        fixed = max(1, used // 4)
        shifted = fixed + (places - fixed + offset_by * (used - fixed)) % max(1, number_of - fixed)
        return jnp.zeros((number_of,), jnp.int32).at[order[jnp.where(places < fixed, places, shifted)]].set(jnp.asarray(sizes, jnp.int32))

    sizes = jnp.where(number % 4 == 0, named(heavy_load, number // 4), named(common, number - number // 4 - 1))
    mixed = jax.random.permutation(jax.random.fold_in(own, 3), number_of)
    giver, receiver = mixed[0:number_of // 2 * 2:2], mixed[1:number_of // 2 * 2:2]
    slack = jnp.minimum(sizes[giver] - 1, most - sizes[receiver]) // 2
    slack = jnp.where((giver == order[0]) | (receiver == order[0]) | (sizes[receiver] == 0), 0, jnp.maximum(slack, 0))
    shifted = jax.random.randint(jax.random.fold_in(own, 4), (number_of // 2,), 0, 1 << 20) % (slack + 1)
    sizes = sizes.at[giver].add(-shifted).at[receiver].add(shifted)
    items = jnp.searchsorted(jnp.cumsum(sizes), jnp.arange(rows * top), side="right").astype(jnp.int32)
    table = items.reshape(top, rows).T
    table = table[jax.random.permutation(jax.random.fold_in(own, 1), rows)]
    offset_by = jax.random.randint(jax.random.fold_in(own, 2), (rows, 1), 0, top)
    return jnp.take_along_axis(table, (jnp.arange(top)[None, :] + offset_by) % top, axis=1)


def portions_of(number_of, total, reach, skew, full):
    weights = [(1 << 20) // math.isqrt(standing ** skew) + 1 for standing in range(1, number_of + 1)]
    largest = reach if full else min(reach, max(-(-total // number_of), total * weights[0] // sum(weights)))
    least = 1 if total - largest >= number_of - 1 else 0
    given, rest = [largest] + [least] * (number_of - 1), total - largest - least * (number_of - 1)
    while rest > 0:
        free = [i for i in range(1, number_of) if given[i] < largest] or [i for i in range(1, number_of) if given[i] < reach]
        whole, remaining = sum([weights[i] for i in free]), rest
        for i in free:
            extra = min(reach - given[i], max(1, remaining * weights[i] // whole), rest)
            given[i] = given[i] + extra
            rest = rest - extra
    return np.array(given)


def bell_draw(rng, dims, width, limit, pieces=(), held_as=jnp.bfloat16):
    array = width * jax.random.normal(rng, dims, jnp.float32)
    if pieces:
        array = array * steps_of(rng, dims, pieces, -0.22, 0.18)
    return jnp.clip(array, -limit, limit).astype(held_as)


def setup_inputs(seed: int = 0) -> dict:
    key_list = jax.random.split(jax.random.key(seed), 10)
    tokens = bell_draw(key_list[0], (ROWS, ROW_TOK, D), 1.0, 6.0, ((0, 32),))
    lengths = plant(jax.random.randint(key_list[1], (ROWS,), 1, ROW_TOK + 1), jax.random.fold_in(key_list[1], 1), 1, ROW_TOK).astype(jnp.int32)
    plan = draw_plan(jax.random.fold_in(key_list[9], 71), 0)
    owners = jax.random.permutation(key_list[3], N_ROLL).astype(jnp.int32)
    gate_up = bell_draw(key_list[4], (N_ROLL, N_TP, D, 2 * FF_WIN), D ** -0.5, 0.125, ((0, 4), (1, 8)), jnp.float32)
    down = bell_draw(key_list[5], (N_ROLL, N_TP, FF_WIN, D), FF_WIN ** -0.5, 0.3125, ((0, 4), (1, 8)), jnp.float32)
    norm_gain = jnp.clip(1.0 + 0.1 * jax.random.normal(key_list[6], (LAYERS, D), jnp.float32), 0.5, 1.5)
    routing_keys = jax.random.split(jax.random.fold_in(key_list[7], 1), LAYERS * (N_ROLL * N_TP * RECV_TOK) // RECV_TOK)
    routing_turns = jax.random.permutation(jax.random.fold_in(key_list[7], 3), LAYERS * (N_ROLL * N_TP * RECV_TOK) // RECV_TOK)
    routing = jax.vmap(lambda own, number: deal_out(jax.random.fold_in(key_list[7], 2), own, number, RECV_TOK, N_TP, 1, CAP_E, 1))(routing_keys, routing_turns).reshape((LAYERS, N_ROLL * N_TP * RECV_TOK, TOPK))
    route_weight = jnp.clip(jnp.exp(math.log(1.0) - 2.3025851 * jax.random.uniform(key_list[8], (LAYERS, N_ROLL * N_TP * RECV_TOK), jnp.float32) ** steps_of(key_list[8], (LAYERS, N_ROLL * N_TP * RECV_TOK), ((1, 32),), -0.2, 0.2)), 0.1, 1.0)
    return {"tokens": tokens, "lengths": lengths, "plan": plan, "owners": owners, "gate_up": gate_up, "down": down, "norm_gain": norm_gain, "routing": routing, "route_weight": route_weight}


epsilon = 1e-06

def expert_apply(normed_rows, gate_up_w, down_w):
    hidden_width = down_w.shape[0]
    projected = jnp.dot(normed_rows, gate_up_w, preferred_element_type=jnp.float32)
    hidden = (jax.nn.silu(projected[:, :hidden_width]) * projected[:, hidden_width:]).astype(jnp.bfloat16)
    return jnp.dot(hidden, down_w, preferred_element_type=jnp.float32).astype(jnp.bfloat16)

def reference(tokens, lengths, plan, owners, gate_up, down, norm_gain, routing, route_weight):
    row_count = tokens.shape[0]
    device_count = N_ROLL * N_TP
    row_index = jnp.arange(row_count, dtype=jnp.int32)
    device_of = row_index // ROWS_DEV
    roll_of = device_of // N_TP
    rank_of = device_of % N_TP
    position = jnp.arange(ROW_TOK, dtype=jnp.int32)
    present = (position[None, :] < lengths[:, None]).astype(jnp.float32).reshape(-1)
    earlier = jnp.arange(ROWS_DEV)[None, :] < jnp.arange(ROWS_DEV)[:, None]
    most_routed = N_ROLL * N_TP * CAP_E
    current = tokens
    for layer_index in range(LAYERS):
        owner_row = plan[layer_index, :, 0]
        grouped = owner_row.reshape(device_count, ROWS_DEV)
        same_owner = grouped[:, :, None] == grouped[:, None, :]
        within = lax.optimization_barrier(jnp.sum(jnp.logical_and(same_owner, earlier[None, :, :]), axis=2)).astype(jnp.int32).reshape(-1)
        target_device = owner_row * N_TP + rank_of
        slot_start = (roll_of * CAP + within) * ROW_TOK
        flat_index = ((target_device * RECV_TOK + slot_start)[:, None] + position[None, :]).reshape(-1).astype(jnp.int32)
        expert_of = routing[layer_index, :, 0][flat_index]
        scale_of = route_weight[layer_index][flat_index]
        widened = current.reshape(-1, D).astype(jnp.float32)
        normed = (widened * lax.rsqrt(lax.optimization_barrier(jnp.mean(widened * widened, axis=1, keepdims=True)) + epsilon) * norm_gain[layer_index][None, :]).astype(jnp.bfloat16)
        owner_index = owners[layer_index]
        layer_gate_up = gate_up[owner_index].astype(jnp.bfloat16)
        layer_down = down[owner_index].astype(jnp.bfloat16)
        token_count = widened.shape[0]

        def add_expert(expert_index, gathered):
            picked = jnp.nonzero(expert_of == expert_index, size=most_routed, fill_value=token_count)[0].astype(jnp.int32)
            rows_in = normed[jnp.minimum(picked, token_count - 1)]
            produced = expert_apply(rows_in, layer_gate_up[expert_index], layer_down[expert_index])
            return gathered.at[picked].set(produced, mode='drop')
        answer = lax.fori_loop(0, N_TP, add_expert, jnp.zeros((token_count, D), jnp.bfloat16))
        combined = widened + (present * scale_of)[:, None] * answer.astype(jnp.float32)
        current = combined.astype(jnp.bfloat16).reshape(row_count, ROW_TOK, D)
    return current
```

```python
import jax
import jax.numpy as jnp
from jax import lax
from jax.sharding import PartitionSpec as P

CAP = 2


epsilon = 1e-06


def spread(block, axis, owner):
    block = jnp.where(lax.axis_index(axis) == owner, block, jnp.zeros_like(block))
    return lax.psum(block, axis)


def slot_plan(target, groups, capacity):
    count = target.shape[0]
    earlier = jnp.arange(count)[None, :] < jnp.arange(count)[:, None]
    same = target[:, None] == target[None, :]
    within = jnp.sum(jnp.logical_and(same, earlier).astype(jnp.int32), axis=1)
    slot = target * capacity + within
    return (jnp.arange(groups * capacity)[:, None] == slot[None, :]).astype(jnp.bfloat16)


def into_slots(taken, items):
    flat = items.reshape(items.shape[0], -1)
    placed = jnp.dot(taken, flat, preferred_element_type=jnp.float32).astype(items.dtype)
    return placed.reshape((-1,) + items.shape[1:])


def from_slots(taken, slots):
    return into_slots(taken.T, slots)


def fetch_layer(gate_up, down, owners, layer_index):
    local_slot = (gate_up[0, 0].astype(jnp.bfloat16), down[0, 0].astype(jnp.bfloat16))
    return (
        spread(local_slot[0], "roll", owners[layer_index]),
        spread(local_slot[1], "roll", owners[layer_index]),
    )


def send_rows_out(current, lengths, taken):
    got_rows = lax.all_to_all(into_slots(taken, current), "roll", split_axis=0, concat_axis=0, tiled=True)
    send_lengths = jnp.sum(jnp.where(taken > 0, lengths[None, :], 0), axis=1)
    got_lengths = lax.all_to_all(send_lengths[:, None], "roll", split_axis=0, concat_axis=0, tiled=True)
    return (got_rows, got_lengths[:, 0])


def send_home(combined, taken):
    home_rows = lax.all_to_all(combined, "roll", split_axis=0, concat_axis=0, tiled=True)
    return from_slots(taken, home_rows)


def process_rows(held, held_lengths, weights, layer_gain, route_column, weight_column):
    tp_size = lax.axis_size("tp")
    row_tokens = held.shape[1]
    model_width = held.shape[2]
    received = held.reshape(-1, model_width)
    token_count = received.shape[0]
    present = (jnp.arange(row_tokens)[None, :] < held_lengths[:, None]).reshape(-1)
    widened = received.astype(jnp.float32)
    normed = (
        widened
        * lax.rsqrt(jnp.mean(widened * widened, axis=1, keepdims=True) + epsilon)
        * layer_gain[None, :]
    ).astype(jnp.bfloat16)
    expert_slots = 5 * token_count // (4 * tp_size)
    taken = slot_plan(route_column, tp_size, expert_slots)
    send_tokens = into_slots(taken, normed).reshape(tp_size, expert_slots, model_width)
    gate_up_w, down_w = weights
    hidden_width = down_w.shape[0]
    arrived = lax.all_to_all(send_tokens, "tp", split_axis=0, concat_axis=0, tiled=True)
    flattened = arrived.reshape(-1, model_width)
    projected = jnp.dot(flattened, gate_up_w, preferred_element_type=jnp.float32)
    hidden = (jax.nn.silu(projected[:, :hidden_width]) * projected[:, hidden_width:]).astype(
        jnp.bfloat16
    )
    produced = jnp.dot(hidden, down_w, preferred_element_type=jnp.float32).astype(jnp.bfloat16)
    returned = lax.all_to_all(
        produced.reshape(arrived.shape), "tp", split_axis=0, concat_axis=0, tiled=True
    )
    answer = from_slots(taken, returned.reshape(-1, model_width))
    combined = (
        widened
        + (present.astype(jnp.float32) * weight_column)[:, None] * answer.astype(jnp.float32)
    ).astype(jnp.bfloat16)
    return combined.reshape(held.shape)


def per_device_wide(tokens, lengths, plan, owners, gate_up, down, norm_gain, routing, route_weight):
    layer_count = plan.shape[0]
    roll_size = lax.axis_size("roll")
    plans = [
        slot_plan(plan[layer_index, :, 0], roll_size, CAP) for layer_index in range(layer_count)
    ]
    current = tokens
    for layer_index in range(layer_count):
        held, held_lengths = send_rows_out(current, lengths, plans[layer_index])
        combined = process_rows(
            held,
            held_lengths,
            fetch_layer(gate_up, down, owners, layer_index),
            norm_gain[layer_index],
            routing[layer_index, :, 0],
            route_weight[layer_index],
        )
        current = send_home(combined, plans[layer_index])
    return current


GATHER_LIMIT = 1 << 23


def token_tables(plan, routing, route_weight, row_tokens, roll_size, tp_size):
    layer_count, rows_dev = plan.shape[0], plan.shape[1]
    slots = routing.shape[1]
    packed = jnp.concatenate(
        [
            plan[:, :, 0].astype(jnp.float32).reshape(-1),
            routing[:, :, 0].astype(jnp.float32).reshape(-1),
            route_weight.reshape(-1),
        ]
    )
    everyone = lax.all_gather(packed, ("roll", "tp"))
    first, second = layer_count * rows_dev, layer_count * (rows_dev + slots)
    owner = everyone[:, :first].reshape(roll_size, tp_size, layer_count, rows_dev)
    owner = owner.astype(jnp.int32).transpose(2, 0, 1, 3)

    def table_of(part):
        part = part.reshape(roll_size, tp_size, layer_count, roll_size, CAP, row_tokens)
        return part.transpose(2, 3, 1, 0, 4, 5)

    expert_table = table_of(everyone[:, first:second])
    weight_table = table_of(everyone[:, second:])
    earlier = jnp.arange(rows_dev)[None, :] < jnp.arange(rows_dev)[:, None]
    same = owner[..., :, None] == owner[..., None, :]
    within = jnp.sum(jnp.logical_and(same, earlier).astype(jnp.int32), axis=-1)
    picks = jnp.logical_and(
        owner[..., None, None] == jnp.arange(roll_size)[:, None],
        within[..., None, None] == jnp.arange(CAP)[None, :],
    )

    def pick(table):
        kept = jnp.where(picks[..., None], table[:, :, :, None], 0.0)
        return jnp.sum(kept, axis=(-3, -2))

    return pick(expert_table).astype(jnp.int32), pick(weight_table)


def per_device_gathered(tokens, lengths, plan, owners, gate_up, down, norm_gain, routing, route_weight):
    layer_count = plan.shape[0]
    roll_size, tp_size = lax.axis_size("roll"), lax.axis_size("tp")
    rows_dev, row_tokens, model_width = tokens.shape
    my_roll, my_tp = lax.axis_index("roll"), lax.axis_index("tp")
    experts, scales = token_tables(plan, routing, route_weight, row_tokens, roll_size, tp_size)
    scales = scales[:, my_roll, my_tp].reshape(layer_count, -1)
    present = (jnp.arange(row_tokens)[None, :] < lengths[:, None]).astype(jnp.float32).reshape(-1)
    gate_up_w, down_w = gate_up[0, 0].astype(jnp.bfloat16), down[0, 0].astype(jnp.bfloat16)
    hidden_width = down_w.shape[0]
    current = tokens.reshape(-1, model_width)
    for layer in range(layer_count):
        widened = current.astype(jnp.float32)
        normed = (
            widened
            * lax.rsqrt(jnp.mean(widened * widened, axis=1, keepdims=True) + epsilon)
            * norm_gain[layer][None, :]
        ).astype(jnp.bfloat16)
        arrived = lax.all_gather(normed, ("roll", "tp"), tiled=True)
        projected = jnp.dot(arrived, gate_up_w, preferred_element_type=jnp.float32)
        hidden = (jax.nn.silu(projected[:, :hidden_width]) * projected[:, hidden_width:]).astype(jnp.bfloat16)
        produced = jnp.dot(hidden, down_w, preferred_element_type=jnp.float32).astype(jnp.bfloat16)
        mine = jnp.logical_and(experts[layer].reshape(-1) == my_tp, owners[layer] == my_roll)
        produced = jnp.where(mine[:, None], produced, jnp.zeros((), produced.dtype))
        answer = lax.psum_scatter(produced, ("roll", "tp"), scatter_dimension=0, tiled=True)
        current = (
            widened + (present * scales[layer])[:, None] * answer.astype(jnp.float32)
        ).astype(jnp.bfloat16)
    return current.reshape(tokens.shape)


def per_device(tokens, *rest):
    devices = lax.axis_size("roll") * lax.axis_size("tp")
    if devices * tokens.size * 2 > GATHER_LIMIT:
        return per_device_wide(tokens, *rest)
    return per_device_gathered(tokens, *rest)


def solution(mesh):
    in_specs = (
        P(("roll", "tp"), None, None),
        P(("roll", "tp")),
        P(None, ("roll", "tp"), None),
        P(),
        P("roll", "tp", None, None),
        P("roll", "tp", None, None),
        P(),
        P(None, ("roll", "tp"), None),
        P(None, ("roll", "tp")),
    )
    out_specs = P(("roll", "tp"), None, None)
    return jax.shard_map(
        per_device, mesh=mesh, in_specs=in_specs, out_specs=out_specs, check_vma=False
    )
```

```python
import jax
import jax.numpy as jnp
from jax import lax
from jax.sharding import PartitionSpec as P

CAP = 2


epsilon = 1e-06


def spread(block, axis, owner):
    block = jnp.where(lax.axis_index(axis) == owner, block, jnp.zeros_like(block))
    return lax.psum(block, axis)


def slot_plan(target, groups, capacity):
    count = target.shape[0]
    earlier = jnp.arange(count)[None, :] < jnp.arange(count)[:, None]
    same = target[:, None] == target[None, :]
    within = jnp.sum(jnp.logical_and(same, earlier).astype(jnp.int32), axis=1)
    slot = target * capacity + within
    return (jnp.arange(groups * capacity)[:, None] == slot[None, :]).astype(jnp.bfloat16)


def into_slots(taken, items):
    flat = items.reshape(items.shape[0], -1)
    placed = jnp.dot(taken, flat, preferred_element_type=jnp.float32).astype(items.dtype)
    return placed.reshape((-1,) + items.shape[1:])


def from_slots(taken, slots):
    return into_slots(taken.T, slots)


def swap(value, distance):
    size = lax.axis_size("roll")
    return lax.ppermute(value, "roll", [(place, place ^ distance) for place in range(size)])


def fetch_layers(gate_up, down, owners, layer_count):
    me = lax.axis_index("roll")
    upper = lax.rem(me, 2) == 1
    kept, given = [], []
    for master in (gate_up[0, 0], down[0, 0]):
        middle = master.shape[0] // 2
        low, high = master[:middle].astype(jnp.bfloat16), master[middle:].astype(jnp.bfloat16)
        kept.append(jnp.where(upper, high, low))
        given.append(jnp.where(upper, low, high))
    got = [swap(half, 1) for half in given]
    layers, before = [], None
    for layer_index in range(layer_count):
        owner = owners[layer_index]
        halves = [
            jnp.where(owner == me, mine, jnp.where(owner == me ^ 1, theirs, jnp.zeros_like(mine)))
            for mine, theirs in zip(kept, got)
        ]
        if before is not None:
            halves, _ = lax.optimization_barrier((halves, before))
        distance = 2
        while distance < lax.axis_size("roll"):
            before = [swap(half, distance) for half in halves]
            halves = [half + other for half, other in zip(halves, before)]
            distance *= 2
        weights = []
        for half in halves:
            other = swap(half, 1)
            weights.append(
                jnp.concatenate([jnp.where(upper, other, half), jnp.where(upper, half, other)], axis=0)
            )
        layers.append(tuple(weights))
    return layers


def send_rows_out(current, lengths, taken):
    got_rows = lax.all_to_all(into_slots(taken, current), "roll", split_axis=0, concat_axis=0, tiled=True)
    send_lengths = jnp.sum(jnp.where(taken > 0, lengths[None, :], 0), axis=1)
    got_lengths = lax.all_to_all(send_lengths[:, None], "roll", split_axis=0, concat_axis=0, tiled=True)
    return (got_rows, got_lengths[:, 0])


def send_home(combined, taken):
    home_rows = lax.all_to_all(combined, "roll", split_axis=0, concat_axis=0, tiled=True)
    return from_slots(taken, home_rows)


def process_rows(held, held_lengths, weights, layer_gain, route_column, weight_column):
    tp_size = lax.axis_size("tp")
    row_tokens = held.shape[1]
    model_width = held.shape[2]
    received = held.reshape(-1, model_width)
    token_count = received.shape[0]
    present = (jnp.arange(row_tokens)[None, :] < held_lengths[:, None]).reshape(-1)
    widened = received.astype(jnp.float32)
    normed = (
        widened
        * lax.rsqrt(jnp.mean(widened * widened, axis=1, keepdims=True) + epsilon)
        * layer_gain[None, :]
    ).astype(jnp.bfloat16)
    expert_slots = 5 * token_count // (4 * tp_size)
    taken = slot_plan(route_column, tp_size, expert_slots)
    send_tokens = into_slots(taken, normed).reshape(tp_size, expert_slots, model_width)
    gate_up_w, down_w = weights
    hidden_width = down_w.shape[0]
    arrived = lax.all_to_all(send_tokens, "tp", split_axis=0, concat_axis=0, tiled=True)
    flattened = arrived.reshape(-1, model_width)
    projected = jnp.dot(flattened, gate_up_w, preferred_element_type=jnp.float32)
    hidden = (jax.nn.silu(projected[:, :hidden_width]) * projected[:, hidden_width:]).astype(
        jnp.bfloat16
    )
    produced = jnp.dot(hidden, down_w, preferred_element_type=jnp.float32).astype(jnp.bfloat16)
    returned = lax.all_to_all(
        produced.reshape(arrived.shape), "tp", split_axis=0, concat_axis=0, tiled=True
    )
    answer = from_slots(taken, returned.reshape(-1, model_width))
    combined = (
        widened
        + (present.astype(jnp.float32) * weight_column)[:, None] * answer.astype(jnp.float32)
    ).astype(jnp.bfloat16)
    return combined.reshape(held.shape)


def per_device(tokens, lengths, plan, owners, gate_up, down, norm_gain, routing, route_weight):
    layer_count = plan.shape[0]
    roll_size = lax.axis_size("roll")
    plans = [
        slot_plan(plan[layer_index, :, 0], roll_size, CAP) for layer_index in range(layer_count)
    ]
    weights = fetch_layers(gate_up, down, owners, layer_count)
    current = tokens
    for layer_index in range(layer_count):
        held, held_lengths = send_rows_out(current, lengths, plans[layer_index])
        combined = process_rows(
            held,
            held_lengths,
            weights[layer_index],
            norm_gain[layer_index],
            routing[layer_index, :, 0],
            route_weight[layer_index],
        )
        current = send_home(combined, plans[layer_index])
    return current


def solution(mesh):
    in_specs = (
        P(("roll", "tp"), None, None),
        P(("roll", "tp")),
        P(None, ("roll", "tp"), None),
        P(),
        P("roll", "tp", None, None),
        P("roll", "tp", None, None),
        P(),
        P(None, ("roll", "tp"), None),
        P(None, ("roll", "tp")),
    )
    out_specs = P(("roll", "tp"), None, None)
    return jax.shard_map(
        per_device, mesh=mesh, in_specs=in_specs, out_specs=out_specs, check_vma=False
    )
```

```python
import jax
import jax.numpy as jnp
from jax import lax
from jax.sharding import PartitionSpec as P

CAP = 2


epsilon = 1e-06


def spread(block, axis, owner):
    block = jnp.where(lax.axis_index(axis) == owner, block, jnp.zeros_like(block))
    return lax.psum(block, axis)


def slot_plan(target, groups, capacity):
    count = target.shape[0]
    earlier = jnp.arange(count)[None, :] < jnp.arange(count)[:, None]
    same = target[:, None] == target[None, :]
    within = jnp.sum(jnp.logical_and(same, earlier).astype(jnp.int32), axis=1)
    slot = target * capacity + within
    return (jnp.arange(groups * capacity)[:, None] == slot[None, :]).astype(jnp.bfloat16)


def into_slots(taken, items):
    flat = items.reshape(items.shape[0], -1)
    placed = jnp.dot(taken, flat, preferred_element_type=jnp.float32).astype(items.dtype)
    return placed.reshape((-1,) + items.shape[1:])


def from_slots(taken, slots):
    return into_slots(taken.T, slots)


def swap(value, distance):
    size = lax.axis_size("roll")
    return lax.ppermute(value, "roll", [(place, place ^ distance) for place in range(size)])


def share_halves(gate_up, down):
    upper = lax.rem(lax.axis_index("roll"), 2) == 1
    kept, given = [], []
    for master in (gate_up[0, 0], down[0, 0]):
        middle = master.shape[0] // 2
        low, high = master[:middle].astype(jnp.bfloat16), master[middle:].astype(jnp.bfloat16)
        kept.append(jnp.where(upper, high, low))
        given.append(jnp.where(upper, low, high))
    return kept, [swap(half, 1) for half in given]


def cross(kept, got, owner, before):
    me = lax.axis_index("roll")
    halves = [
        jnp.where(owner == me, mine, jnp.where(owner == me ^ 1, theirs, jnp.zeros_like(mine)))
        for mine, theirs in zip(kept, got)
    ]
    if before is not None:
        halves, _ = lax.optimization_barrier((halves, before))
    others = [jnp.zeros_like(half) for half in halves]
    distance = 2
    while distance < lax.axis_size("roll"):
        halves = [half + other for half, other in zip(halves, others)] if distance > 2 else halves
        others = [swap(half, distance) for half in halves]
        distance *= 2
    return halves, others


def complete(halves, others):
    upper = lax.rem(lax.axis_index("roll"), 2) == 1
    weights = []
    for half, other in zip(halves, others):
        half = half + other
        other = swap(half, 1)
        weights.append(
            jnp.concatenate([jnp.where(upper, other, half), jnp.where(upper, half, other)], axis=0)
        )
    return weights


def share_plan(plan, lengths, roll_size):
    layer_count, rows_dev = plan.shape[0], plan.shape[1]
    packed = jnp.concatenate([plan[:, :, 0].reshape(-1), lengths])
    sent = jnp.broadcast_to(packed[None, :], (roll_size, packed.shape[0]))
    got = lax.all_to_all(sent, "roll", split_axis=0, concat_axis=0, tiled=True)
    return got[:, :-rows_dev].reshape(roll_size, layer_count, rows_dev), got[:, -rows_dev:]


def held_lengths(owner, row_lengths):
    me, count = lax.axis_index("roll"), owner.shape[1]
    earlier = jnp.arange(count)[None, :] < jnp.arange(count)[:, None]
    same = owner[:, :, None] == owner[:, None, :]
    within = jnp.sum(jnp.logical_and(same, earlier[None]).astype(jnp.int32), axis=2)
    here = jnp.logical_and(
        (owner == me)[:, None, :], within[:, None, :] == jnp.arange(CAP)[None, :, None]
    )
    return jnp.sum(jnp.where(here, row_lengths[:, None, :], 0), axis=2).reshape(-1)


def forward_plan(previous, owner, roll_size):
    me = lax.axis_index("roll")
    homes = jnp.arange(roll_size)
    turned = lax.rem(owner - homes[:, None] + roll_size, roll_size)
    turn = jnp.max(
        jnp.where(previous[:, :, None] == homes[None, None, :], turned[:, :, None], -1), axis=(0, 1)
    )
    mine = jnp.max(jnp.where(homes == me, turn, -1))
    to_send = jnp.logical_and(mine >= 0, homes[:, None] == lax.rem(homes[None, :] + mine, roll_size))
    to_keep = jnp.logical_and(turn[None, :] >= 0, lax.rem(homes[:, None] + turn[None, :], roll_size) == me)
    return to_send.astype(jnp.bfloat16), to_keep.astype(jnp.bfloat16)


def forward_rows(combined, moves, roll_size):
    chunks = into_slots(moves[0], combined.reshape((roll_size, CAP) + combined.shape[1:]))
    came = lax.all_to_all(chunks, "roll", split_axis=0, concat_axis=0, tiled=True)
    return into_slots(moves[1], came).reshape(combined.shape)


def send_home(combined, taken):
    home_rows = lax.all_to_all(combined, "roll", split_axis=0, concat_axis=0, tiled=True)
    return from_slots(taken, home_rows)


def process_rows(held, slot_lengths, crossing, first, layer_gain, route_column, weight_column):
    tp_size = lax.axis_size("tp")
    row_tokens = held.shape[1]
    model_width = held.shape[2]
    received = held.reshape(-1, model_width)
    token_count = received.shape[0]
    present = (jnp.arange(row_tokens)[None, :] < slot_lengths[:, None]).reshape(-1)
    widened = received.astype(jnp.float32)
    normed = (
        widened
        * lax.rsqrt(jnp.mean(widened * widened, axis=1, keepdims=True) + epsilon)
        * layer_gain[None, :]
    ).astype(jnp.bfloat16)
    expert_slots = 5 * token_count // (4 * tp_size)
    taken = slot_plan(route_column, tp_size, expert_slots)
    send_tokens = into_slots(taken, normed).reshape(tp_size, expert_slots, model_width)
    arrived = lax.all_to_all(send_tokens, "tp", split_axis=0, concat_axis=0, tiled=True)
    halves, others = crossing
    if first:
        others, arrived = lax.optimization_barrier((others, arrived))
    gate_up_w, down_w = complete(halves, others)
    hidden_width = down_w.shape[0]
    flattened = arrived.reshape(-1, model_width)
    projected = jnp.dot(flattened, gate_up_w, preferred_element_type=jnp.float32)
    hidden = (jax.nn.silu(projected[:, :hidden_width]) * projected[:, hidden_width:]).astype(
        jnp.bfloat16
    )
    produced = jnp.dot(hidden, down_w, preferred_element_type=jnp.float32).astype(jnp.bfloat16)
    returned = lax.all_to_all(
        produced.reshape(arrived.shape), "tp", split_axis=0, concat_axis=0, tiled=True
    )
    answer = from_slots(taken, returned.reshape(-1, model_width))
    combined = (
        widened
        + (present.astype(jnp.float32) * weight_column)[:, None] * answer.astype(jnp.float32)
    ).astype(jnp.bfloat16)
    return combined.reshape(held.shape)


def per_device(tokens, lengths, plan, owners, gate_up, down, norm_gain, routing, route_weight):
    layer_count = plan.shape[0]
    roll_size = lax.axis_size("roll")
    kept, got = share_halves(gate_up, down)
    home = slot_plan(plan[layer_count - 1, :, 0], roll_size, CAP)
    owner, row_lengths = share_plan(plan, lengths, roll_size)
    first_rows = into_slots(slot_plan(plan[0, :, 0], roll_size, CAP), tokens)
    held = lax.all_to_all(first_rows, "roll", split_axis=0, concat_axis=0, tiled=True)
    crossings, before = [], None
    for layer_index in range(layer_count):
        crossings.append(cross(kept, got, owners[layer_index], before))
        before = crossings[-1][1]
    for layer_index in range(layer_count):
        if layer_index > 0:
            moves = forward_plan(owner[:, layer_index - 1], owner[:, layer_index], roll_size)
            held = forward_rows(held, moves, roll_size)
        held = process_rows(
            held,
            held_lengths(owner[:, layer_index], row_lengths),
            crossings[layer_index],
            layer_index == 0,
            norm_gain[layer_index],
            routing[layer_index, :, 0],
            route_weight[layer_index],
        )
    current = send_home(held, home)
    return current


def solution(mesh):
    in_specs = (
        P(("roll", "tp"), None, None),
        P(("roll", "tp")),
        P(None, ("roll", "tp"), None),
        P(),
        P("roll", "tp", None, None),
        P("roll", "tp", None, None),
        P(),
        P(None, ("roll", "tp"), None),
        P(None, ("roll", "tp")),
    )
    out_specs = P(("roll", "tp"), None, None)
    return jax.shard_map(
        per_device, mesh=mesh, in_specs=in_specs, out_specs=out_specs, check_vma=False
    )
```

```python
import jax
import jax.numpy as jnp
from jax import lax
from jax.sharding import PartitionSpec as P

CAP = 2


epsilon = 1e-06


def spread(block, axis, owner):
    block = jnp.where(lax.axis_index(axis) == owner, block, jnp.zeros_like(block))
    return lax.psum(block, axis)


def slot_plan(target, groups, capacity):
    count = target.shape[0]
    earlier = jnp.arange(count)[None, :] < jnp.arange(count)[:, None]
    same = target[:, None] == target[None, :]
    within = jnp.sum(jnp.logical_and(same, earlier).astype(jnp.int32), axis=1)
    slot = target * capacity + within
    return (jnp.arange(groups * capacity)[:, None] == slot[None, :]).astype(jnp.bfloat16)


def into_slots(taken, items):
    flat = items.reshape(items.shape[0], -1)
    placed = jnp.dot(taken, flat, preferred_element_type=jnp.float32).astype(items.dtype)
    return placed.reshape((-1,) + items.shape[1:])


def from_slots(taken, slots):
    return into_slots(taken.T, slots)


def swap(value, distance):
    size = lax.axis_size("roll")
    return lax.ppermute(value, "roll", [(place, place ^ distance) for place in range(size)])


def share_halves(gate_up, down):
    upper = lax.rem(lax.axis_index("roll"), 2) == 1
    kept, given = [], []
    for master in (gate_up[0, 0], down[0, 0]):
        middle = master.shape[0] // 2
        low, high = master[:middle].astype(jnp.bfloat16), master[middle:].astype(jnp.bfloat16)
        kept.append(jnp.where(upper, high, low))
        given.append(jnp.where(upper, low, high))
    return kept, [swap(half, 1) for half in given]


def cross(kept, got, owner, before):
    me = lax.axis_index("roll")
    halves = [
        jnp.where(owner == me, mine, jnp.where(owner == me ^ 1, theirs, jnp.zeros_like(mine)))
        for mine, theirs in zip(kept, got)
    ]
    halves, _ = lax.optimization_barrier((halves, before))
    others = [jnp.zeros_like(half) for half in halves]
    distance = 2
    while distance < lax.axis_size("roll"):
        halves = [half + other for half, other in zip(halves, others)] if distance > 2 else halves
        others = [swap(half, distance) for half in halves]
        distance *= 2
    return halves, others


def complete(halves, others):
    upper = lax.rem(lax.axis_index("roll"), 2) == 1
    weights = []
    for half, other in zip(halves, others):
        half = half + other
        other = swap(half, 1)
        weights.append(
            jnp.concatenate([jnp.where(upper, other, half), jnp.where(upper, half, other)], axis=0)
        )
    return weights


def share_plan(plan, lengths, roll_size):
    layer_count, rows_dev = plan.shape[0], plan.shape[1]
    packed = jnp.concatenate([plan[:, :, 0].reshape(-1), lengths])
    sent = jnp.broadcast_to(packed[None, :], (roll_size, packed.shape[0]))
    got = lax.all_to_all(sent, "roll", split_axis=0, concat_axis=0, tiled=True)
    return got[:, :-rows_dev].reshape(roll_size, layer_count, rows_dev), got[:, -rows_dev:]


def held_lengths(owner, row_lengths):
    me, count = lax.axis_index("roll"), owner.shape[1]
    earlier = jnp.arange(count)[None, :] < jnp.arange(count)[:, None]
    same = owner[:, :, None] == owner[:, None, :]
    within = jnp.sum(jnp.logical_and(same, earlier[None]).astype(jnp.int32), axis=2)
    here = jnp.logical_and(
        (owner == me)[:, None, :], within[:, None, :] == jnp.arange(CAP)[None, :, None]
    )
    return jnp.sum(jnp.where(here, row_lengths[:, None, :], 0), axis=2).reshape(-1)


def forward_plan(previous, owner, roll_size):
    me = lax.axis_index("roll")
    homes = jnp.arange(roll_size)
    turned = lax.rem(owner - homes[:, None] + roll_size, roll_size)
    turn = jnp.max(
        jnp.where(previous[:, :, None] == homes[None, None, :], turned[:, :, None], -1), axis=(0, 1)
    )
    mine = jnp.max(jnp.where(homes == me, turn, -1))
    to_send = jnp.logical_and(mine >= 0, homes[:, None] == lax.rem(homes[None, :] + mine, roll_size))
    to_keep = jnp.logical_and(turn[None, :] >= 0, lax.rem(homes[:, None] + turn[None, :], roll_size) == me)
    return to_send.astype(jnp.bfloat16), to_keep.astype(jnp.bfloat16)


def forward_rows(combined, moves, roll_size):
    chunks = into_slots(moves[0], combined.reshape((roll_size, CAP) + combined.shape[1:]))
    came = lax.all_to_all(chunks, "roll", split_axis=0, concat_axis=0, tiled=True)
    return into_slots(moves[1], came).reshape(combined.shape)


def send_home(combined, taken):
    home_rows = lax.all_to_all(combined, "roll", split_axis=0, concat_axis=0, tiled=True)
    return from_slots(taken, home_rows)


def process_rows(held, slot_lengths, crossing, first, layer_gain, route_column, weight_column):
    tp_size = lax.axis_size("tp")
    row_tokens = held.shape[1]
    model_width = held.shape[2]
    received = held.reshape(-1, model_width)
    token_count = received.shape[0]
    present = (jnp.arange(row_tokens)[None, :] < slot_lengths[:, None]).reshape(-1)
    widened = received.astype(jnp.float32)
    normed = (
        widened
        * lax.rsqrt(jnp.mean(widened * widened, axis=1, keepdims=True) + epsilon)
        * layer_gain[None, :]
    ).astype(jnp.bfloat16)
    expert_slots = 5 * token_count // (4 * tp_size)
    taken = slot_plan(route_column, tp_size, expert_slots)
    send_tokens = into_slots(taken, normed).reshape(tp_size, expert_slots, model_width)
    arrived = lax.all_to_all(send_tokens, "tp", split_axis=0, concat_axis=0, tiled=True)
    halves, others = crossing
    if first:
        others, arrived = lax.optimization_barrier((others, arrived))
    gate_up_w, down_w = complete(halves, others)
    hidden_width = down_w.shape[0]
    flattened = arrived.reshape(-1, model_width)
    projected = jnp.dot(flattened, gate_up_w, preferred_element_type=jnp.float32)
    hidden = (jax.nn.silu(projected[:, :hidden_width]) * projected[:, hidden_width:]).astype(
        jnp.bfloat16
    )
    produced = jnp.dot(hidden, down_w, preferred_element_type=jnp.float32).astype(jnp.bfloat16)
    returned = lax.all_to_all(
        produced.reshape(arrived.shape), "tp", split_axis=0, concat_axis=0, tiled=True
    )
    answer = from_slots(taken, returned.reshape(-1, model_width))
    combined = (
        widened
        + (present.astype(jnp.float32) * weight_column)[:, None] * answer.astype(jnp.float32)
    ).astype(jnp.bfloat16)
    return combined.reshape(held.shape)


def per_device(tokens, lengths, plan, owners, gate_up, down, norm_gain, routing, route_weight):
    layer_count = plan.shape[0]
    roll_size = lax.axis_size("roll")
    kept, got = share_halves(gate_up, down)
    home = slot_plan(plan[layer_count - 1, :, 0], roll_size, CAP)
    owner, row_lengths = share_plan(plan, lengths, roll_size)
    first_rows = into_slots(slot_plan(plan[0, :, 0], roll_size, CAP), tokens)
    held = lax.all_to_all(first_rows, "roll", split_axis=0, concat_axis=0, tiled=True)
    crossings, before = [], (owner, row_lengths, held)
    for layer_index in range(layer_count):
        crossings.append(cross(kept, got, owners[layer_index], before))
        before = crossings[-1][1]
    for layer_index in range(layer_count):
        if layer_index > 0:
            moves = forward_plan(owner[:, layer_index - 1], owner[:, layer_index], roll_size)
            held = forward_rows(held, moves, roll_size)
        held = process_rows(
            held,
            held_lengths(owner[:, layer_index], row_lengths),
            crossings[layer_index],
            layer_index == 0,
            norm_gain[layer_index],
            routing[layer_index, :, 0],
            route_weight[layer_index],
        )
    current = send_home(held, home)
    return current


def solution(mesh):
    in_specs = (
        P(("roll", "tp"), None, None),
        P(("roll", "tp")),
        P(None, ("roll", "tp"), None),
        P(),
        P("roll", "tp", None, None),
        P("roll", "tp", None, None),
        P(),
        P(None, ("roll", "tp"), None),
        P(None, ("roll", "tp")),
    )
    out_specs = P(("roll", "tp"), None, None)
    return jax.shard_map(
        per_device, mesh=mesh, in_specs=in_specs, out_specs=out_specs, check_vma=False
    )
```
